768 devices in a mesh: group: 24 (over z, core), sub: 32 (over y, x).
Axes of the slice: x: 4, y: 8, z: 12, core: 2. Of those that a mesh axis runs over, the one named last changes fastest.
Arguments:
- load: float32 [8, 12288, 256], P(None, ('group', 'sub'))
- row_scale: float32 [12288, 256], P(('group', 'sub'))
- diag_blocks: bfloat16 [12288, 256, 256], P(('group', 'sub')), may hold values from -0.01184082 to 0.01184082
- off_blocks: bfloat16 [12288, 256, 256], P(('group', 'sub')), may hold values from -0.01184082 to 0.01184082
- off_pattern: int32 [768, 16], P(('group', 'sub')), may hold values from 0 to 15, each once within a row
- partner: int32 [768, 16], P(('group', 'sub')), may hold values from 0 to 31, as said below
- corner_coupling: bfloat16 [6144, 4096], P(('group', 'sub')), may hold values from -0.375 to 0.375
- corner_index: int32 [24, 256], P('group'), may hold values from 0 to 127
- coarse_inverse: float32 [3072, 128], P('group'), as said below
Outputs:
- multipliers: float32 [8, 12288, 256], P(None, ('group', 'sub'))
- residual: float32 [8, 12288, 256], P(None, ('group', 'sub'))
The draws below stay inside these ranges and needn't reach their ends.
Inputs may be any that keep to these rules, and one draw needn't show every extreme that they name: partner[s, i] is t XOR m for the subdomain s = 32 * grp + t, with m nonzero and depending only on grp and i; so block i of s and block i of its partner share one multiplier. No subdomain shares more than 1 block with one other subdomain, and some share exactly 1. `coarse_inverse`: each cluster's block is symmetric and positive definite.
All inputs are finite; a program needn't handle non-finite values.
Results may differ from the reference program's by a relative error of at most 0.012.
The reference program's roundings to bfloat16 on the way (of `scaled` and `local`) count: a program that leaves them out, or rounds other values in their place, can miss the bound.
Values sent between devices are 32-bit elements; how exact they have to be, the bound alone decides.
A program may use at most 32 MiB of HBM per device.

```python
import jax
import jax.numpy as jnp
from jax import lax

BS = 256
NB = 16
NC = 8
NRHS = 8
ITERS = 4
SUBS = 768
CG = 128
CAP = 1
N_GROUP = 24
N_SUB = 32


def draw_partner(key, part):
    key = jax.random.fold_in(key, 11)

    def one_group(index):
        group_key = jax.random.fold_in(key, index)
        order = jax.random.permutation(jax.random.fold_in(group_key, 1), N_SUB - 1).astype(jnp.int32) + 1
        tiled = jnp.tile(order, CAP)[:NB]
        place = jax.random.permutation(jax.random.fold_in(group_key, 2), NB)
        return tiled[place]
    masks = jax.vmap(one_group)(jnp.arange(N_GROUP, dtype=jnp.int32))
    local = jnp.arange(N_SUB, dtype=jnp.int32)
    mates = jnp.bitwise_xor(local[None, :, None], masks[:, None, :])
    return mates.reshape(N_GROUP * N_SUB, NB).astype(jnp.int32)


def place_in_cluster():
    within = jnp.arange(SUBS * NB, dtype=jnp.int32) // NB % N_SUB
    return within.astype(jnp.float32) / (N_SUB - 1) - 0.5


def draw_load(key, part):
    key = jax.random.fold_in(key, 12)
    place = place_in_cluster()
    base = jax.random.normal(key, (NRHS, SUBS * NB, BS), jnp.float32)
    grow = 3.0 ** place
    return base * grow[None, :, None]


def draw_row_scale(key, part):
    key = jax.random.fold_in(key, 14)
    place = place_in_cluster()
    base = jnp.exp(jax.random.uniform(key, (SUBS * NB, BS), jnp.float32, -0.5, 0.47))
    fall = 3.0 ** (-place)
    return base * fall[:, None]


def draw_coarse_inverse(key, part):
    key = jax.random.fold_in(key, 13)
    reach = 0.9 / CG
    raw = jax.random.uniform(key, (N_GROUP, CG, CG), jnp.float32, -reach, reach)
    mirrored = 0.5 * (raw + jnp.swapaxes(raw, 1, 2))
    eye = jnp.eye(CG, dtype=jnp.float32)[None]
    return (0.5 * (eye + mirrored)).reshape(N_GROUP * CG, CG)


def plant(drawn, rng, least, largest):
    index_at = [jax.random.randint(jax.random.fold_in(rng, axis), (), 0, length) for axis, length in enumerate(drawn.shape)]
    widest = drawn.shape.index(max(drawn.shape))
    beside = index_at[:widest] + [(index_at[widest] + 1) % drawn.shape[widest]] + index_at[widest + 1:]
    return drawn.at[tuple(index_at)].set(least).at[tuple(beside)].set(largest)


def block_scale(stream_key, dims, shards, low, high):
    def one(dim, shards_of):
        heights = jax.random.uniform(jax.random.fold_in(jax.random.fold_in(stream_key, 6), dim), (shards_of,), jnp.float32, low / len(shards), high / len(shards))
        return jnp.repeat(jnp.exp(heights), dims[dim] // shards_of).reshape((-1,) + (1,) * (len(dims) - dim - 1))

    gain = one(*shards[0])
    for cut in shards[1:]:
        gain = gain * one(*cut)
    return gain


def centred(rng, shape, width, most, cuts=(), kind=jnp.bfloat16):
    entries = width * jax.random.normal(rng, shape, jnp.float32)
    if cuts:
        entries = entries * block_scale(rng, shape, cuts, -0.22, 0.18)
    return jnp.clip(entries, -most, most).astype(kind)


def setup_inputs(seed: int = 0) -> dict:
    seeds = jax.random.split(jax.random.key(seed), 10)
    return {
        "load": draw_load(jax.random.fold_in(seeds[9], 71), 0),
        "row_scale": draw_row_scale(jax.random.fold_in(seeds[9], 71), 0),
        "diag_blocks": jnp.clip(jax.random.uniform(seeds[2], (SUBS * NB, BS, BS), jnp.float32, -0.01184082, 0.01184082) * block_scale(seeds[2], (SUBS * NB, BS, BS), ((0, 768),), -0.4, 0.0), -0.01184082, 0.01184082).astype(jnp.bfloat16),
        "off_blocks": jnp.clip(jax.random.uniform(seeds[3], (SUBS * NB, BS, BS), jnp.float32, -0.01184082, 0.01184082) * block_scale(seeds[3], (SUBS * NB, BS, BS), ((0, 768),), -0.4, 0.0), -0.01184082, 0.01184082).astype(jnp.bfloat16),
        "off_pattern": jax.vmap(lambda own: jax.random.permutation(own, NB))(jax.random.split(seeds[4], SUBS)).reshape((SUBS, NB)).astype(jnp.int32),
        "partner": draw_partner(jax.random.fold_in(seeds[9], 71), 0),
        "corner_coupling": centred(seeds[6], (SUBS * NC, NB * BS), BS ** -0.5, 0.375, ((0, 768),)),
        "corner_index": plant(jax.random.randint(seeds[7], (N_GROUP, N_SUB * NC), 0, CG), jax.random.fold_in(seeds[7], 1), 0, CG - 1).astype(jnp.int32),
        "coarse_inverse": draw_coarse_inverse(jax.random.fold_in(seeds[9], 71), 0),
    }


HIGH = lax.Precision.HIGHEST


def couple(args):
    diag, off, sigma, vals = args
    kd = diag.astype(jnp.float32)
    ko = off.astype(jnp.float32)
    values = vals.astype(jnp.float32)
    select = (sigma[:, None] == jnp.arange(NB, dtype=jnp.int32)[None, :]).astype(jnp.float32)
    moved = jnp.einsum("ij,njl->nil", select, values, precision=HIGH)
    total = jnp.einsum("ikl,nil->nik", kd, values, precision=HIGH)
    total = total + jnp.einsum("ilk,nil->nik", kd, values, precision=HIGH)
    total = total + jnp.einsum("ikl,nil->nik", ko, moved, precision=HIGH)
    back = jnp.einsum("ilk,nil->nik", ko, values, precision=HIGH)
    return total + jnp.einsum("ij,nik->njk", select, back, precision=HIGH)


def reference(load, row_scale, diag_blocks, off_blocks, off_pattern, partner, corner_coupling, corner_index, coarse_inverse):
    scale = row_scale.reshape(SUBS, NB, BS)
    diag = diag_blocks.reshape(SUBS, NB, BS, BS)
    off = off_blocks.reshape(SUBS, NB, BS, BS)
    coupling = corner_coupling.reshape(SUBS, NC, NB * BS).astype(jnp.float32)
    base = (jnp.arange(SUBS, dtype=jnp.int32) // N_SUB) * N_SUB
    mate = base[:, None] + partner
    slot = jnp.broadcast_to(jnp.arange(NB, dtype=jnp.int32)[None, :], (SUBS, NB))
    onehot = (corner_index[:, :, None] == jnp.arange(CG, dtype=jnp.int32)[None, None, :]).astype(jnp.float32)
    inverse = coarse_inverse.reshape(N_GROUP, CG, CG)

    def jump(field):
        return field - field[:, mate, slot, :]

    def apply(field):
        scaled = (scale[None] * field).astype(jnp.bfloat16)
        coupled = lax.map(couple, (diag, off, off_pattern, jnp.transpose(scaled, (1, 0, 2, 3))))
        coupled = jnp.transpose(coupled, (1, 0, 2, 3))
        flat = scaled.astype(jnp.float32).reshape(NRHS, SUBS, NB * BS)
        partial_terms = jnp.einsum("scr,nsr->nsc", coupling, flat, precision=HIGH)
        grouped = partial_terms.reshape(NRHS, N_GROUP, N_SUB * NC)
        gathered = jnp.einsum("gjc,ngj->ngc", onehot, grouped, precision=HIGH)
        solved = jnp.einsum("gcd,ngd->ngc", inverse, gathered, precision=HIGH)
        local = jnp.einsum("gjc,ngc->ngj", onehot, solved, precision=HIGH).astype(jnp.bfloat16)
        local = local.reshape(NRHS, SUBS, NC).astype(jnp.float32)
        lifted = jnp.einsum("scr,nsc->nsr", coupling, local, precision=HIGH).reshape(NRHS, SUBS, NB, BS)
        return jump(scale[None] * (scaled.astype(jnp.float32) + coupled + lifted))

    def column(first, second):
        return jnp.sum(first * second, axis=(1, 2, 3))

    field = load.reshape(NRHS, SUBS, NB, BS)
    residual = jump(field)
    multipliers = jnp.zeros_like(residual)
    direction = residual
    norm_now = column(residual, residual)
    for step in range(ITERS):
        product = apply(direction)
        alpha = norm_now / column(direction, product)
        multipliers = multipliers + alpha[:, None, None, None] * direction
        residual = residual - alpha[:, None, None, None] * product
        norm_next = column(residual, residual)
        direction = residual + (norm_next / norm_now)[:, None, None, None] * direction
        norm_now = norm_next
    return multipliers.reshape(NRHS, SUBS * NB, BS), residual.reshape(NRHS, SUBS * NB, BS)
```

```python
import jax
import jax.numpy as jnp
from jax import lax
from jax.experimental import pallas as pl
from jax.experimental.pallas import tpu as pltpu
from jax.sharding import PartitionSpec as P

ITERS = 4
MESH = pl.DeviceIdType.MESH
F32 = jnp.float32
BF16 = jnp.bfloat16


def dot(a, b):
    return jnp.dot(a, b, preferred_element_type=F32)


def split(x):
    high = x.astype(BF16)
    return high, (x - high.astype(F32)).astype(BF16)


def iota(shape, axis):
    return lax.broadcasted_iota(jnp.int32, shape, axis)


def kernel(
    load_hbm,
    scale_hbm,
    diag_hbm,
    off_hbm,
    pattern_hbm,
    partner_hbm,
    coupling_hbm,
    index_hbm,
    inverse_hbm,
    mult_ref,
    res_ref,
    load_ref,
    scale_ref,
    diag,
    off,
    pattern_ref,
    partner_ref,
    coupling_ref,
    index_ref,
    inverse_ref,
    basis,
    image,
    field,
    stacked,
    back,
    coarse_rows,
    coarse_wide,
    lift_high,
    lift_low,
    lift,
    onehot,
    pick,
    local,
    info,
    norms,
    ritzes,
    direction,
    residual,
    multipliers,
    squares,
    landing,
    slot_block,
    block_slot,
    inverse_pattern,
    row_send,
    dot_send,
    group_send,
    send,
    recv,
    row_recv,
    dot_recv,
    group_recv,
    local_sem,
    send_sem,
    row_send_sem,
    dot_send_sem,
    group_send_sem,
    recv_sem,
    row_sem,
    dot_sem,
    group_sem,
):
    groups = lax.axis_size("group")
    peers = lax.axis_size("sub")
    group = lax.axis_index("group")
    me = lax.axis_index("sub")
    blocks = 16
    corners = 8

    pairs = (
        (partner_hbm, partner_ref),
        (pattern_hbm, pattern_ref),
        (load_hbm, load_ref),
        (scale_hbm, scale_ref),
        (coupling_hbm, coupling_ref),
        (index_hbm, index_ref),
        (inverse_hbm, inverse_ref),
        (diag_hbm, diag),
        (off_hbm, off),
    )
    copies = [pltpu.make_async_copy(a, b, local_sem.at[k]) for k, (a, b) in enumerate(pairs)]
    for copy in copies:
        copy.start()

    barrier = pltpu.get_barrier_semaphore()

    @pl.loop(1, peers)
    def _(o):
        pl.semaphore_signal(
            barrier, inc=1, device_id={"sub": lax.rem(me + o, peers)}, device_id_type=MESH
        )

    @pl.loop(1, groups)
    def _(o):
        pl.semaphore_signal(
            barrier, inc=1, device_id={"group": lax.rem(group + o, groups)}, device_id_type=MESH
        )

    def all_offsets(body):
        @pl.loop(0, peers - 4)
        def _(s):
            q = s // 4
            far = 4 + ((q + 1) // 2) * (1 - 2 * (q % 2))
            body(4 * far + s % 4)

        @pl.loop(1, 4)
        def _(o):
            body(o)

    def swap_field(source, number):
        def one(o):
            send[number, o] = source[slot_block[o]]
            pltpu.make_async_remote_copy(
                src_ref=send.at[number, o],
                dst_ref=recv.at[number, o],
                send_sem=send_sem.at[number],
                recv_sem=recv_sem.at[number],
                device_id={"sub": lax.rem(me + o, peers)},
                device_id_type=MESH,
            ).start()

        all_offsets(one)

    def wait_field(number):
        rest = pl.ds(1, peers - 1)
        ref = recv.at[number, rest]
        pltpu.make_async_copy(ref, ref, recv_sem.at[number]).wait()
        ref = send.at[number, rest]
        pltpu.make_async_copy(ref, ref, send_sem.at[number]).wait()
        for o in range(1, 32):
            landing[o] = recv[number, o]

    def swap_row(row, source, target, step, out_sem, in_sem):
        source[step] = row
        target[step, 0] = row

        def one(o):
            pltpu.make_async_remote_copy(
                src_ref=source.at[step],
                dst_ref=target.at[step, o],
                send_sem=out_sem.at[step],
                recv_sem=in_sem.at[step],
                device_id={"sub": lax.rem(me + o, peers)},
                device_id_type=MESH,
            ).start()

        all_offsets(one)

    def wait_row(target, step, out_sem, in_sem):
        ref = target.at[step, pl.ds(1, peers - 1)]
        pltpu.make_async_copy(ref, ref, in_sem.at[step]).wait()
        pltpu.make_async_copy(ref, ref, out_sem.at[step]).wait()

    lane = iota((8, 128), 1)
    sub = iota((8, 128), 0)

    def to_row(columns):
        total = jnp.zeros((8, 128), F32)
        for k, c in enumerate(columns):
            total = jnp.where(lane // 8 == k, c, total)
        return jnp.sum(jnp.where(lane % 8 == sub, total, 0.0), axis=0, keepdims=True)

    def to_column(row):
        return jnp.sum(jnp.where(lane == sub, row, 0.0), axis=1, keepdims=True)

    def over(top, bottom, other):
        return jnp.where(bottom > 0.0, top / jnp.where(bottom > 0.0, bottom, 1.0), other)

    def wide(row):
        return jnp.broadcast_to(row, (8, 128))

    def swap_group(row, number):
        group_send[number] = row
        group_recv[number, 0] = row

        @pl.loop(1, groups)
        def _(o):
            pltpu.make_async_remote_copy(
                src_ref=group_send.at[number],
                dst_ref=group_recv.at[number, o],
                send_sem=group_send_sem.at[number],
                recv_sem=group_sem.at[number],
                device_id={"group": lax.rem(group + o, groups)},
                device_id_type=MESH,
            ).start()

    def wait_group(number):
        ref = group_recv.at[number, pl.ds(1, groups - 1)]
        pltpu.make_async_copy(ref, ref, group_sem.at[number]).wait()
        pltpu.make_async_copy(ref, ref, group_send_sem.at[number]).wait()
        return group_recv[number].reshape(groups, 128)

    def positive(ritz):
        return jnp.where(ritz == 0.0, 1.0, jnp.abs(ritz))

    def advance():
        d = [direction[j] for j in range(ITERS + 1)]
        weight = [norms[j] for j in range(ITERS)]
        a = [ritzes[j] for j in range(ITERS)]
        product = [a[j] * d[j] for j in range(ITERS)] + [jnp.zeros_like(d[0])]
        for j in range(ITERS):
            growth = positive(a[j])
            product[j + 1] = product[j + 1] + growth * d[j]
            if j < ITERS - 1:
                product[j] = product[j] + over(weight[j + 1] * growth, weight[j], 0.0) * d[j + 1]

        def total(left, right):
            value = weight[0] * left[0] * right[0]
            for j in range(1, ITERS):
                value = value + weight[j] * left[j] * right[j]
            return jnp.sum(value, axis=0, keepdims=True)

        now = squares[0:1]
        alpha = now / total(d, product)
        r = [residual[j] - alpha * product[j] for j in range(ITERS + 1)]
        after = total(r, r)
        ratio = after / now
        for j in range(ITERS + 1):
            multipliers[j] = multipliers[j] + alpha * d[j]
            residual[j] = r[j]
            direction[j] = r[j] + ratio * d[j]
        squares[...] = wide(after)

    def own(value):
        return to_column(value[0:1])

    for copy in copies[:2]:
        copy.wait()

    @pl.loop(1, peers)
    def _(o):
        peer = lax.rem(me + o, peers)
        found = jnp.int32(0)
        for i in range(blocks):
            found = jnp.where(partner_ref[0, i] == peer, jnp.int32(i), found)
        slot_block[o] = found

    @pl.loop(0, blocks)
    def _(i):
        found = jnp.int32(0)
        for j in range(blocks):
            found = jnp.where(pattern_ref[0, j] == i, jnp.int32(j), found)
        inverse_pattern[i] = found
        block_slot[i] = lax.rem(me - partner_ref[0, i] + peers, peers)

    for copy in copies[2:5]:
        copy.wait()
    for i in range(blocks):
        field[i] = load_ref[:, i, :]
        scale = scale_ref[i : i + 1, :]
        coarse_rows[i] = coupling_ref[:, 256 * i : 256 * (i + 1)].astype(F32) * scale

    pl.semaphore_wait(barrier, peers - 1 + groups - 1)
    swap_field(field, 0)
    swap_field(coarse_rows, 1)

    for j in range(corners):
        for i in range(blocks):
            row = coupling_ref[:, 256 * i : 256 * (i + 1)].astype(F32)[j : j + 1]
            coarse_wide[j, i] = jnp.broadcast_to(row, (8, 256))
    for copy in copies[5:7]:
        copy.wait()
    natural = (index_ref[...] == iota((128, 256), 0)).astype(BF16)
    p = iota((256, 256), 0)
    q = iota((256, 256), 1)
    order = ((p // 8 == (me - q % 32 + 32) % 32) & (p % 8 == q // 32)).astype(F32).astype(BF16)
    onehot[...] = dot(natural, order).astype(BF16)
    mate = iota((1, 256), 1)
    owner = jnp.zeros((1, 256), jnp.int32) + me
    for i in range(blocks):
        owner = jnp.where((mate // 16 == i) & (mate % 16 >= 8), partner_ref[0, i], owner)
    sign = jnp.where(q % 16 >= 8, -1.0, 1.0)
    choose = jnp.where((p // 8 == owner) & (p % 8 == q % 8), sign, 0.0).astype(BF16)
    pick[...] = dot(natural, choose).astype(BF16)
    for ref in (local, norms, ritzes, direction, residual, multipliers):
        ref[...] = jnp.zeros_like(ref)
    direction[0] = jnp.ones_like(direction[0])
    residual[0] = jnp.ones_like(residual[0])
    for copy in copies[7:]:
        copy.wait()

    @pl.loop(0, blocks)
    def _(i):
        half = diag[i].astype(F32)
        diag[i] = (half + half.T).astype(BF16)

    wait_field(0)
    for i in range(blocks):
        basis[0, i] = field[i] - landing[block_slot[i]]

    @pl.loop(0, ITERS)
    def _(step):
        before = jnp.maximum(step - 1, 0)
        parts = [jnp.zeros((8, 256), F32) for _ in range(corners + 1)]
        for i in range(blocks):
            v = basis[step, i]
            scaled = scale_ref[i : i + 1, :] * v
            high = scaled.astype(BF16).astype(F32)
            scaled = jnp.where(step == 0, high, scaled)
            field[i] = scaled
            stacked[i] = jnp.concatenate([high, scaled - high], axis=0).astype(BF16)
            for j in range(corners):
                parts[j] = parts[j] + scaled * coarse_wide[j, i]
            parts[corners] = parts[corners] + v * v
        row = to_row([jnp.sum(part, axis=1, keepdims=True) for part in parts])
        swap_row(row, row_send, row_recv, step, row_send_sem, row_sem)

        for i in range(blocks):
            x = stacked[i]
            behind = dot(x, off[i])
            back[i] = behind[:8] + behind[8:]
            ahead = dot(x, diag[i]) + lax.dot_general(
                stacked[pattern_ref[0, i]],
                off[i],
                (((1,), (1,)), ((), ())),
                preferred_element_type=F32,
            )
            image[i] = ahead[:8] + ahead[8:]
        product = jnp.zeros((8, 256), F32)
        for i in range(blocks):
            scale = scale_ref[i : i + 1, :]
            scaled = field[i]
            total = scaled + image[i] + back[inverse_pattern[i]]
            product = product + scale * basis[step, i] * total
            image[i] = scale * total
        row = to_row([jnp.sum(product, axis=1, keepdims=True)])
        swap_row(row, dot_send, dot_recv, step, dot_send_sem, dot_sem)
        swap_field(image, step + 2)

        @pl.when(step == 0)
        def _():
            wait_field(1)
            for i in range(blocks):
                rows = jnp.concatenate([coarse_rows[i], landing[block_slot[i]]], axis=0)
                high, low = split(rows)
                lift_high[16 * i : 16 * (i + 1), :] = high
                lift_low[16 * i : 16 * (i + 1), :] = low

        wait_row(row_recv, step, row_send_sem, row_sem)
        rows = row_recv[step].reshape(peers, 128)
        norm = pltpu.roll(wide(jnp.sum(rows, axis=0, keepdims=True)), 64, 1)
        info[step] = norm

        @pl.when(step > 0)
        def _():
            kinds = (info[before], pltpu.roll(norm, 8, 1), pltpu.roll(info[4 + before], 16, 1))
            row = jnp.zeros((8, 128), F32)
            for k, value in enumerate(kinds):
                row = jnp.where(lane // 8 == k, value, row)
            swap_group(row[:1], before)

        high, low = split(
            jnp.concatenate(
                [rows] + [pltpu.roll(rows, 128 - 8 * j, 1) for j in range(1, corners)], axis=0
            )
        )
        gathered = dot(onehot[...], high) + dot(onehot[...], low)
        high, low = split(gathered)
        inverse_high, inverse_low = split(inverse_ref[...])
        solved = dot(inverse_high, high) + (dot(inverse_high, low) + dot(inverse_low, high))
        energy = jnp.sum(gathered * solved, axis=0, keepdims=True)
        high, low = split(solved.T[:8])
        both = jnp.concatenate([high.astype(F32), low.astype(F32)], axis=0).astype(BF16)
        both = dot(both, pick[...])
        local[step] = both[:8] + both[8:]

        wait_row(dot_recv, step, dot_send_sem, dot_sem)
        rows = dot_recv[step].reshape(peers, 128)
        ritz = over(2.0 * wide(jnp.sum(rows, axis=0, keepdims=True) + energy), norm, 0.0)
        old = over(norm * positive(info[4 + before]), info[before], 0.0)
        old = jnp.where(step > 0, old, 0.0)
        info[4 + step] = ritz

        @pl.when(step == ITERS - 1)
        def _():
            swap_group(ritz[:1], ITERS - 1)

        @pl.when(step > 0)
        def _():
            rows = wait_group(before)

            @pl.when(step == 1)
            def _():
                norms[0] = rows
                squares[...] = wide(jnp.sum(rows, axis=0, keepdims=True))

            norms[step] = pltpu.roll(rows, 120, 1)
            ritzes[before] = pltpu.roll(rows, 112, 1)
            advance()

        exact = jnp.zeros((8, 256), F32)
        for j in range(ITERS):
            exact = exact + own(direction[j]) * local[j]
        share = own(direction[step])
        slip = exact.astype(BF16).astype(F32) - exact
        slip = jnp.where(share == 0.0, 0.0, slip / jnp.where(share == 0.0, 1.0, share))
        value = local[step] + slip
        spread = jnp.concatenate(
            [jnp.where(iota((8, 256), 1) // 16 == i, value, 0.0) for i in range(blocks)], axis=0
        )
        high, low = split(spread)
        lift[...] = dot(high, lift_high[...]) + (dot(low, lift_high[...]) + dot(high, lift_low[...]))

        shrink = to_column(1.0 / positive(ritz))
        ritz = to_column(ritz)
        old = to_column(old)
        wait_field(step + 2)
        for i in range(blocks):
            jumped = image[i] - landing[block_slot[i]] + lift[8 * i : 8 * (i + 1), :]
            basis[step + 1, i] = (jumped - ritz * basis[step, i] - old * basis[before, i]) * shrink

    ritzes[ITERS - 1] = wait_group(ITERS - 1)
    advance()
    weights = [own(multipliers[j]) for j in range(ITERS)]
    shares = [own(residual[j]) for j in range(ITERS + 1)]
    for i in range(blocks):
        vectors = [basis[j, i] for j in range(ITERS + 1)]
        value = weights[0] * vectors[0]
        for j in range(1, ITERS):
            value = value + weights[j] * vectors[j]
        mult_ref[i] = value
        value = shares[0] * vectors[0]
        for j in range(1, ITERS + 1):
            value = value + shares[j] * vectors[j]
        res_ref[i] = value


def on_device(
    load,
    row_scale,
    diag_blocks,
    off_blocks,
    off_pattern,
    partner,
    corner_coupling,
    corner_index,
    coarse_inverse,
):
    groups = lax.axis_size("group")
    peers = lax.axis_size("sub")
    vmem = pl.BlockSpec(memory_space=pltpu.VMEM)
    dma = pltpu.SemaphoreType.DMA
    field = jax.ShapeDtypeStruct((16, 8, 256), F32)
    multipliers, residual = pl.pallas_call(
        kernel,
        out_shape=(field, field),
        in_specs=[pl.BlockSpec(memory_space=pl.ANY)] * 9,
        out_specs=(vmem, vmem),
        scratch_shapes=[
            pltpu.VMEM(load.shape, F32),
            pltpu.VMEM(row_scale.shape, F32),
            pltpu.VMEM(diag_blocks.shape, BF16),
            pltpu.VMEM(off_blocks.shape, BF16),
            pltpu.SMEM(off_pattern.shape, jnp.int32),
            pltpu.SMEM(partner.shape, jnp.int32),
            pltpu.VMEM(corner_coupling.shape, BF16),
            pltpu.VMEM(corner_index.shape, jnp.int32),
            pltpu.VMEM(coarse_inverse.shape, F32),
            pltpu.VMEM((ITERS + 1, 16, 8, 256), F32),
            pltpu.VMEM((16, 8, 256), F32),
            pltpu.VMEM((16, 8, 256), F32),
            pltpu.VMEM((16, 16, 256), BF16),
            pltpu.VMEM((16, 8, 256), F32),
            pltpu.VMEM((16, 8, 256), F32),
            pltpu.VMEM((8, 16, 8, 256), F32),
            pltpu.VMEM((256, 256), BF16),
            pltpu.VMEM((256, 256), BF16),
            pltpu.VMEM((128, 256), F32),
            pltpu.VMEM((128, 256), BF16),
            pltpu.VMEM((128, 256), BF16),
            pltpu.VMEM((ITERS, 8, 256), F32),
            pltpu.VMEM((2 * ITERS, 8, 128), F32),
            pltpu.VMEM((ITERS, groups, 128), F32),
            pltpu.VMEM((ITERS, groups, 128), F32),
            pltpu.VMEM((ITERS + 1, groups, 128), F32),
            pltpu.VMEM((ITERS + 1, groups, 128), F32),
            pltpu.VMEM((ITERS + 1, groups, 128), F32),
            pltpu.VMEM((8, 128), F32),
            pltpu.VMEM((peers, 8, 256), F32),
            pltpu.SMEM((32,), jnp.int32),
            pltpu.SMEM((16,), jnp.int32),
            pltpu.SMEM((16,), jnp.int32),
            pltpu.VMEM((ITERS, 1, 128), F32),
            pltpu.VMEM((ITERS, 1, 128), F32),
            pltpu.VMEM((ITERS, 1, 128), F32),
            pltpu.VMEM((ITERS + 2, 32, 8, 256), F32),
            pltpu.VMEM((ITERS + 2, 32, 8, 256), F32),
            pltpu.VMEM((ITERS, 32, 1, 128), F32),
            pltpu.VMEM((ITERS, 32, 1, 128), F32),
            pltpu.VMEM((ITERS, groups, 1, 128), F32),
            dma((9,)),
            dma((ITERS + 2,)),
            dma((ITERS,)),
            dma((ITERS,)),
            dma((ITERS,)),
            dma((ITERS + 2,)),
            dma((ITERS,)),
            dma((ITERS,)),
            dma((ITERS,)),
        ],
        compiler_params=pltpu.CompilerParams(
            collective_id=0, has_side_effects=True, vmem_limit_bytes=63 * 2**20
        ),
    )(
        load,
        row_scale,
        diag_blocks,
        off_blocks,
        off_pattern,
        partner,
        corner_coupling,
        corner_index,
        coarse_inverse,
    )
    return jnp.transpose(multipliers, (1, 0, 2)), jnp.transpose(residual, (1, 0, 2))


def solution(mesh):
    return jax.shard_map(
        on_device,
        mesh=mesh,
        in_specs=(
            P(None, ("group", "sub"), None),
            P(("group", "sub"), None),
            P(("group", "sub"), None, None),
            P(("group", "sub"), None, None),
            P(("group", "sub"), None),
            P(("group", "sub"), None),
            P(("group", "sub"), None),
            P("group", None),
            P("group", None),
        ),
        out_specs=(P(None, ("group", "sub"), None), P(None, ("group", "sub"), None)),
        check_vma=False,
    )
```

```python
import jax
import jax.numpy as jnp
from jax import lax
from jax.experimental import pallas as pl
from jax.experimental.pallas import tpu as pltpu
from jax.sharding import PartitionSpec as P

ITERS = 4
MESH = pl.DeviceIdType.MESH
F32 = jnp.float32
BF16 = jnp.bfloat16


def dot(a, b):
    return jnp.dot(a, b, preferred_element_type=F32)


def split(x):
    high = x.astype(BF16)
    return high, (x - high.astype(F32)).astype(BF16)


def product(x, matrix):
    high = x.astype(BF16)
    low = x - high.astype(F32)
    both = jnp.concatenate([high.astype(F32), low], axis=0).astype(BF16)
    value = dot(both, matrix)
    return value[: x.shape[0]] + value[x.shape[0] :], high


def iota(shape, axis):
    return lax.broadcasted_iota(jnp.int32, shape, axis)


def kernel(
    load_hbm,
    scale_hbm,
    diag_hbm,
    off_hbm,
    pattern_hbm,
    partner_hbm,
    coupling_hbm,
    index_hbm,
    inverse_hbm,
    mult_ref,
    res_ref,
    load_ref,
    scale_ref,
    diag,
    off,
    pattern_ref,
    partner_ref,
    coupling_ref,
    index_ref,
    inverse_ref,
    basis,
    image,
    field,
    stacked,
    back,
    coarse_rows,
    coarse_wide,
    lift_high,
    lift_low,
    lift,
    onehot,
    inverse_high,
    inverse_low,
    reply_high,
    reply_low,
    local,
    info,
    norms,
    ritzes,
    direction,
    residual,
    multipliers,
    squares,
    landing,
    slot_block,
    block_slot,
    inverse_pattern,
    row_send,
    dot_send,
    group_send,
    send,
    recv,
    row_recv,
    dot_recv,
    group_recv,
    local_sem,
    send_sem,
    row_send_sem,
    dot_send_sem,
    group_send_sem,
    recv_sem,
    row_sem,
    dot_sem,
    group_sem,
):
    groups = lax.axis_size("group")
    peers = lax.axis_size("sub")
    group = lax.axis_index("group")
    me = lax.axis_index("sub")
    blocks = 16
    corners = 8

    pairs = (
        (partner_hbm, partner_ref),
        (load_hbm, load_ref),
        (pattern_hbm, pattern_ref),
        (scale_hbm, scale_ref),
        (coupling_hbm, coupling_ref),
        (index_hbm, index_ref),
        (inverse_hbm, inverse_ref),
        (diag_hbm, diag),
        (off_hbm, off),
    )
    copies = [pltpu.make_async_copy(a, b, local_sem.at[k]) for k, (a, b) in enumerate(pairs)]
    for copy in copies:
        copy.start()

    barrier = pltpu.get_barrier_semaphore()

    @pl.loop(1, peers)
    def _(o):
        pl.semaphore_signal(
            barrier, inc=1, device_id={"sub": lax.rem(me + o, peers)}, device_id_type=MESH
        )

    @pl.loop(1, groups)
    def _(o):
        pl.semaphore_signal(
            barrier, inc=1, device_id={"group": lax.rem(group + o, groups)}, device_id_type=MESH
        )

    def all_offsets(body):
        for far in (4, 3, 5, 2, 6, 1, 7):
            for s in range(4):
                body(4 * far + s)
        for o in range(1, 4):
            body(o)

    def swap_field(source, number):
        def one(o):
            send[number, o] = source[slot_block[o]]
            pltpu.make_async_remote_copy(
                src_ref=send.at[number, o],
                dst_ref=recv.at[number, o],
                send_sem=send_sem.at[number],
                recv_sem=recv_sem.at[number],
                device_id={"sub": lax.rem(me + o, peers)},
                device_id_type=MESH,
            ).start()

        all_offsets(one)

    def wait_field(number):
        rest = pl.ds(1, peers - 1)
        ref = recv.at[number, rest]
        pltpu.make_async_copy(ref, ref, recv_sem.at[number]).wait()
        ref = send.at[number, rest]
        pltpu.make_async_copy(ref, ref, send_sem.at[number]).wait()
        for o in range(1, 32):
            landing[o] = recv[number, o]

    def swap_row(row, source, target, step, out_sem, in_sem):
        source[step] = row
        target[step, 0] = row

        def one(o):
            pltpu.make_async_remote_copy(
                src_ref=source.at[step],
                dst_ref=target.at[step, o],
                send_sem=out_sem.at[step],
                recv_sem=in_sem.at[step],
                device_id={"sub": lax.rem(me + o, peers)},
                device_id_type=MESH,
            ).start()

        all_offsets(one)

    def wait_row(target, step, out_sem, in_sem):
        ref = target.at[step, pl.ds(1, peers - 1)]
        pltpu.make_async_copy(ref, ref, in_sem.at[step]).wait()
        pltpu.make_async_copy(ref, ref, out_sem.at[step]).wait()

    lane = iota((8, 128), 1)
    sub = iota((8, 128), 0)

    def to_row(columns):
        total = jnp.zeros((8, 128), F32)
        for k, c in enumerate(columns):
            total = jnp.where(lane // 8 == k, c, total)
        return jnp.sum(jnp.where(lane % 8 == sub, total, 0.0), axis=0, keepdims=True)

    def to_column(row):
        return jnp.sum(jnp.where(lane == sub, row, 0.0), axis=1, keepdims=True)

    def over(top, bottom, other):
        return jnp.where(bottom > 0.0, top / jnp.where(bottom > 0.0, bottom, 1.0), other)

    def wide(row):
        return jnp.broadcast_to(row, (8, 128))

    def swap_group(row, number):
        group_send[number] = row
        group_recv[number, 0] = row

        @pl.loop(1, groups)
        def _(o):
            pltpu.make_async_remote_copy(
                src_ref=group_send.at[number],
                dst_ref=group_recv.at[number, o],
                send_sem=group_send_sem.at[number],
                recv_sem=group_sem.at[number],
                device_id={"group": lax.rem(group + o, groups)},
                device_id_type=MESH,
            ).start()

    def wait_group(number):
        ref = group_recv.at[number, pl.ds(1, groups - 1)]
        pltpu.make_async_copy(ref, ref, group_sem.at[number]).wait()
        pltpu.make_async_copy(ref, ref, group_send_sem.at[number]).wait()
        return group_recv[number].reshape(groups, 128)

    def positive(ritz):
        return jnp.where(ritz == 0.0, 1.0, jnp.abs(ritz))

    def advance():
        d = [direction[j] for j in range(ITERS + 1)]
        weight = [norms[j] for j in range(ITERS)]
        a = [ritzes[j] for j in range(ITERS)]
        product = [a[j] * d[j] for j in range(ITERS)] + [jnp.zeros_like(d[0])]
        for j in range(ITERS):
            growth = positive(a[j])
            product[j + 1] = product[j + 1] + growth * d[j]
            if j < ITERS - 1:
                product[j] = product[j] + over(weight[j + 1] * growth, weight[j], 0.0) * d[j + 1]

        def total(left, right):
            value = weight[0] * left[0] * right[0]
            for j in range(1, ITERS):
                value = value + weight[j] * left[j] * right[j]
            return jnp.sum(value, axis=0, keepdims=True)

        now = squares[0:1]
        alpha = now / total(d, product)
        r = [residual[j] - alpha * product[j] for j in range(ITERS + 1)]
        after = total(r, r)
        ratio = after / now
        for j in range(ITERS + 1):
            multipliers[j] = multipliers[j] + alpha * d[j]
            residual[j] = r[j]
            direction[j] = r[j] + ratio * d[j]
        squares[...] = wide(after)

    def own(value):
        return to_column(value[0:1])

    copies[0].wait()
    mates = [partner_ref[0, i] for i in range(blocks)]

    @pl.loop(1, peers)
    def _(o):
        peer = lax.rem(me + o, peers)
        found = jnp.int32(0)
        for i in range(blocks):
            found = jnp.where(mates[i] == peer, jnp.int32(i), found)
        slot_block[o] = found

    copies[1].wait()
    for i in range(blocks):
        field[i] = load_ref[:, i, :]

    pl.semaphore_wait(barrier, peers - 1 + groups - 1)
    swap_field(field, 0)
    for copy in copies[2:5]:
        copy.wait()
    for i in range(blocks):
        scale = scale_ref[i : i + 1, :]
        coarse_rows[i] = coupling_ref[:, 256 * i : 256 * (i + 1)].astype(F32) * scale
    swap_field(coarse_rows, 1)

    @pl.loop(0, blocks)
    def _(i):
        found = jnp.int32(0)
        for j in range(blocks):
            found = jnp.where(pattern_ref[0, j] == i, jnp.int32(j), found)
        inverse_pattern[i] = found
        block_slot[i] = lax.rem(me - partner_ref[0, i] + peers, peers)

    for j in range(corners):
        for i in range(blocks):
            row = coupling_ref[:, 256 * i : 256 * (i + 1)].astype(F32)[j : j + 1]
            coarse_wide[j, i] = jnp.broadcast_to(row, (8, 256))
    for copy in copies[5:7]:
        copy.wait()
    natural = (index_ref[...] == iota((128, 256), 0)).astype(BF16)
    p = iota((256, 256), 0)
    q = iota((256, 256), 1)
    order = ((q // 8 == (me - p % 32 + 32) % 32) & (q % 8 == p // 32)).astype(F32).astype(BF16)
    place = lax.dot_general(order, natural, (((1,), (1,)), ((), ())), preferred_element_type=F32)
    onehot[...] = place.astype(BF16)
    mate = iota((1, 256), 1)
    owner = jnp.zeros((1, 256), jnp.int32) + me
    for i in range(blocks):
        owner = jnp.where((mate // 16 == i) & (mate % 16 >= 8), partner_ref[0, i], owner)
    sign = jnp.where(q % 16 >= 8, -1.0, 1.0)
    choose = jnp.where((p // 8 == owner) & (p % 8 == q % 8), sign, 0.0).astype(BF16)
    pick = dot(natural, choose).astype(BF16)
    high, low = split(inverse_ref[...].T)
    inverse_high[...] = high
    inverse_low[...] = low
    for part, ref in ((high, reply_high), (low, reply_low)):
        picked = dot(part, pick).astype(BF16)
        ref[...] = dot(onehot[...], picked).astype(BF16)
    for ref in (local, norms, ritzes, direction, residual, multipliers):
        ref[...] = jnp.zeros_like(ref)
    direction[0] = jnp.ones_like(direction[0])
    residual[0] = jnp.ones_like(residual[0])
    for copy in copies[7:]:
        copy.wait()

    @pl.loop(0, blocks)
    def _(i):
        half = diag[i].astype(F32)
        diag[i] = (half + half.T).astype(BF16)

    wait_field(0)
    for i in range(blocks):
        basis[0, i] = field[i] - landing[block_slot[i]]

    @pl.loop(0, ITERS)
    def _(step):
        before = jnp.maximum(step - 1, 0)
        parts = [jnp.zeros((8, 256), F32) for _ in range(corners + 1)]
        for i in range(blocks):
            v = basis[step, i]
            scaled = scale_ref[i : i + 1, :] * v
            high = scaled.astype(BF16).astype(F32)
            scaled = jnp.where(step == 0, high, scaled)
            field[i] = scaled
            stacked[i] = jnp.concatenate([high, scaled - high], axis=0).astype(BF16)
            for j in range(corners):
                parts[j] = parts[j] + scaled * coarse_wide[j, i]
            parts[corners] = parts[corners] + v * v
        row = to_row([jnp.sum(part, axis=1, keepdims=True) for part in parts])
        swap_row(row, row_send, row_recv, step, row_send_sem, row_sem)

        for i in range(blocks):
            x = stacked[i]
            behind = dot(x, off[i])
            back[i] = behind[:8] + behind[8:]
            ahead = dot(x, diag[i]) + lax.dot_general(
                stacked[pattern_ref[0, i]],
                off[i],
                (((1,), (1,)), ((), ())),
                preferred_element_type=F32,
            )
            image[i] = ahead[:8] + ahead[8:]
        inner = jnp.zeros((8, 256), F32)
        for i in range(blocks):
            scale = scale_ref[i : i + 1, :]
            scaled = field[i]
            total = scaled + image[i] + back[inverse_pattern[i]]
            inner = inner + scale * basis[step, i] * total
            image[i] = scale * total
        row = to_row([jnp.sum(inner, axis=1, keepdims=True)])
        swap_row(row, dot_send, dot_recv, step, dot_send_sem, dot_sem)
        swap_field(image, step + 2)

        @pl.when(step == 0)
        def _():
            wait_field(1)
            for i in range(blocks):
                rows = jnp.concatenate([coarse_rows[i], landing[block_slot[i]]], axis=0)
                high, low = split(rows)
                lift_high[16 * i : 16 * (i + 1), :] = high
                lift_low[16 * i : 16 * (i + 1), :] = low

        wait_row(row_recv, step, row_send_sem, row_sem)
        rows = row_recv[step].reshape(peers, 128)
        norm = pltpu.roll(wide(jnp.sum(rows, axis=0, keepdims=True)), 64, 1)
        info[step] = norm

        @pl.when(step > 0)
        def _():
            kinds = (info[before], pltpu.roll(norm, 8, 1), pltpu.roll(info[4 + before], 16, 1))
            row = jnp.zeros((8, 128), F32)
            for k, value in enumerate(kinds):
                row = jnp.where(lane // 8 == k, value, row)
            swap_group(row[:1], before)

        turned = jnp.concatenate([rows, jnp.zeros((128 - 32, 128), F32)], axis=0).T
        sides = []
        for half in range(2):
            side = turned[32 * half : 32 * half + 8]
            for k in range(1, 4):
                piece = turned[32 * half + 8 * k : 32 * half + 8 * (k + 1)]
                side = side + pltpu.roll(piece, 32 * k, 1)
            sides.append(side)
        partials = jnp.concatenate(sides, axis=1)
        value, high = product(partials, reply_high[...])
        local[step] = value + dot(high, reply_low[...])
        gathered, _ = product(partials, onehot[...])
        solved, high = product(gathered, inverse_high[...])
        solved = solved + dot(high, inverse_low[...])
        energy = to_row([jnp.sum(gathered * solved, axis=1, keepdims=True)])
        old = over(norm * positive(info[4 + before]), info[before], 0.0)
        old = jnp.where(step > 0, old, 0.0)

        def ritz_value():
            wait_row(dot_recv, step, dot_send_sem, dot_sem)
            rows = dot_recv[step].reshape(peers, 128)
            ritz = over(2.0 * wide(jnp.sum(rows, axis=0, keepdims=True) + energy), norm, 0.0)
            info[4 + step] = ritz
            return ritz

        @pl.when(step == ITERS - 1)
        def _():
            swap_group(ritz_value()[:1], ITERS - 1)

        @pl.when(step > 0)
        def _():
            rows = wait_group(before)

            @pl.when(step == 1)
            def _():
                norms[0] = rows
                squares[...] = wide(jnp.sum(rows, axis=0, keepdims=True))

            norms[step] = pltpu.roll(rows, 120, 1)
            ritzes[before] = pltpu.roll(rows, 112, 1)
            advance()

        exact = jnp.zeros((8, 256), F32)
        for j in range(ITERS):
            exact = exact + own(direction[j]) * local[j]
        share = own(direction[step])
        slip = exact.astype(BF16).astype(F32) - exact
        slip = jnp.where(share == 0.0, 0.0, slip / jnp.where(share == 0.0, 1.0, share))
        value = local[step] + slip
        spread = jnp.concatenate(
            [jnp.where(iota((8, 256), 1) // 16 == i, value, 0.0) for i in range(blocks)], axis=0
        )
        high, low = split(spread)
        lift[...] = dot(high, lift_high[...]) + (dot(low, lift_high[...]) + dot(high, lift_low[...]))

        @pl.when(step < ITERS - 1)
        def _():
            ritz_value()

        ritz = info[4 + step]
        shrink = to_column(1.0 / positive(ritz))
        ritz = to_column(ritz)
        old = to_column(old)
        wait_field(step + 2)
        for i in range(blocks):
            jumped = image[i] - landing[block_slot[i]] + lift[8 * i : 8 * (i + 1), :]
            basis[step + 1, i] = (jumped - ritz * basis[step, i] - old * basis[before, i]) * shrink

    ritzes[ITERS - 1] = wait_group(ITERS - 1)
    advance()
    weights = [own(multipliers[j]) for j in range(ITERS)]
    shares = [own(residual[j]) for j in range(ITERS + 1)]
    for i in range(blocks):
        vectors = [basis[j, i] for j in range(ITERS + 1)]
        value = weights[0] * vectors[0]
        for j in range(1, ITERS):
            value = value + weights[j] * vectors[j]
        mult_ref[i] = value
        value = shares[0] * vectors[0]
        for j in range(1, ITERS + 1):
            value = value + shares[j] * vectors[j]
        res_ref[i] = value


def turn(a_ref, b_ref, c_ref, d_ref):
    for i in range(a_ref.shape[0]):
        c_ref[:, i, :] = a_ref[i]
        d_ref[:, i, :] = b_ref[i]


def on_device(
    load,
    row_scale,
    diag_blocks,
    off_blocks,
    off_pattern,
    partner,
    corner_coupling,
    corner_index,
    coarse_inverse,
):
    groups = lax.axis_size("group")
    peers = lax.axis_size("sub")
    vmem = pl.BlockSpec(memory_space=pltpu.VMEM)
    dma = pltpu.SemaphoreType.DMA
    field = jax.ShapeDtypeStruct((16, 8, 256), F32)
    multipliers, residual = pl.pallas_call(
        kernel,
        out_shape=(field, field),
        in_specs=[pl.BlockSpec(memory_space=pl.ANY)] * 9,
        out_specs=(vmem, vmem),
        scratch_shapes=[
            pltpu.VMEM(load.shape, F32),
            pltpu.VMEM(row_scale.shape, F32),
            pltpu.VMEM(diag_blocks.shape, BF16),
            pltpu.VMEM(off_blocks.shape, BF16),
            pltpu.SMEM(off_pattern.shape, jnp.int32),
            pltpu.SMEM(partner.shape, jnp.int32),
            pltpu.VMEM(corner_coupling.shape, BF16),
            pltpu.VMEM(corner_index.shape, jnp.int32),
            pltpu.VMEM(coarse_inverse.shape, F32),
            pltpu.VMEM((ITERS + 1, 16, 8, 256), F32),
            pltpu.VMEM((16, 8, 256), F32),
            pltpu.VMEM((16, 8, 256), F32),
            pltpu.VMEM((16, 16, 256), BF16),
            pltpu.VMEM((16, 8, 256), F32),
            pltpu.VMEM((16, 8, 256), F32),
            pltpu.VMEM((8, 16, 8, 256), F32),
            pltpu.VMEM((256, 256), BF16),
            pltpu.VMEM((256, 256), BF16),
            pltpu.VMEM((128, 256), F32),
            pltpu.VMEM((256, 128), BF16),
            pltpu.VMEM((128, 128), BF16),
            pltpu.VMEM((128, 128), BF16),
            pltpu.VMEM((256, 256), BF16),
            pltpu.VMEM((256, 256), BF16),
            pltpu.VMEM((ITERS, 8, 256), F32),
            pltpu.VMEM((2 * ITERS, 8, 128), F32),
            pltpu.VMEM((ITERS, groups, 128), F32),
            pltpu.VMEM((ITERS, groups, 128), F32),
            pltpu.VMEM((ITERS + 1, groups, 128), F32),
            pltpu.VMEM((ITERS + 1, groups, 128), F32),
            pltpu.VMEM((ITERS + 1, groups, 128), F32),
            pltpu.VMEM((8, 128), F32),
            pltpu.VMEM((peers, 8, 256), F32),
            pltpu.SMEM((32,), jnp.int32),
            pltpu.SMEM((16,), jnp.int32),
            pltpu.SMEM((16,), jnp.int32),
            pltpu.VMEM((ITERS, 1, 128), F32),
            pltpu.VMEM((ITERS, 1, 128), F32),
            pltpu.VMEM((ITERS, 1, 128), F32),
            pltpu.VMEM((ITERS + 2, 32, 8, 256), F32),
            pltpu.VMEM((ITERS + 2, 32, 8, 256), F32),
            pltpu.VMEM((ITERS, 32, 1, 128), F32),
            pltpu.VMEM((ITERS, 32, 1, 128), F32),
            pltpu.VMEM((ITERS, groups, 1, 128), F32),
            dma((9,)),
            dma((ITERS + 2,)),
            dma((ITERS,)),
            dma((ITERS,)),
            dma((ITERS,)),
            dma((ITERS + 2,)),
            dma((ITERS,)),
            dma((ITERS,)),
            dma((ITERS,)),
        ],
        compiler_params=pltpu.CompilerParams(
            collective_id=0, has_side_effects=True, vmem_limit_bytes=63 * 2**20
        ),
    )(
        load,
        row_scale,
        diag_blocks,
        off_blocks,
        off_pattern,
        partner,
        corner_coupling,
        corner_index,
        coarse_inverse,
    )
    turned = jax.ShapeDtypeStruct(load.shape, F32)
    return pl.pallas_call(
        turn,
        out_shape=(turned, turned),
        in_specs=[vmem, vmem],
        out_specs=(vmem, vmem),
    )(multipliers, residual)


def solution(mesh):
    return jax.shard_map(
        on_device,
        mesh=mesh,
        in_specs=(
            P(None, ("group", "sub"), None),
            P(("group", "sub"), None),
            P(("group", "sub"), None, None),
            P(("group", "sub"), None, None),
            P(("group", "sub"), None),
            P(("group", "sub"), None),
            P(("group", "sub"), None),
            P("group", None),
            P("group", None),
        ),
        out_specs=(P(None, ("group", "sub"), None), P(None, ("group", "sub"), None)),
        check_vma=False,
    )
```
